32 devices in a mesh: ctx: 4 (over z), head: 4 (over x, core), side: 2 (over y).
Axes of the slice: x: 2, y: 2, z: 4, core: 2. Of those that a mesh axis runs over, the one named last changes fastest.
Arguments:
- prefill_query: bfloat16 [1024, 64, 128], P('ctx', ('head', 'side')), may hold values from -6 to 6
- prefill_keys: bfloat16 [1024, 8, 128], P('ctx', ('head', 'side')), may hold values from -6 to 6
- prefill_values: bfloat16 [1024, 8, 128], P('ctx', ('head', 'side')), may hold values from -6 to 6
- token_pos: int32 [1024], P('ctx'), may hold values from 0 to 1023, as said below
- scale_exp: int32 [16, 8, 2], P('ctx', ('head', 'side')), may hold values from -7 to -5
- page_owner: int32 [16], P('ctx'), may hold values from 0 to 3, as said below
- draft_query: bfloat16 [256, 64, 128], P(None, ('head', 'side')), may hold values from -6 to 6
- draft_keys: bfloat16 [256, 8, 128], P('side', 'head'), may hold values from -6 to 6
- draft_values: bfloat16 [256, 8, 128], P('side', 'head'), may hold values from -6 to 6
- parents: int32 [256], replicated, may hold values from 0 to 254, as said below
Outputs:
- prefill_out: bfloat16 [1024, 64, 128], P('ctx', ('head', 'side'))
- cache_keys: bfloat16 [1024, 8, 128], P('ctx', ('head', 'side'))
- cache_values: bfloat16 [1024, 8, 128], P('ctx', ('head', 'side'))
- verify_out: bfloat16 [256, 64, 128], P('ctx', ('head', 'side'))
The draws below stay inside these ranges and needn't reach their ends.
Inputs may be any that keep to these rules, and one draw needn't show every extreme that they name: `token_pos`: a permutation of 0 to 1023; the rows of shard c of ctx hold the runs a and 2 * 4 - 1 - a of 128 consecutive positions, in order, with a different a for each shard. `page_owner`: the 16 // 4 entries of one ctx shard are a permutation of 0 to 4 - 1. parents[0] = 0, and parents[r] < r for r >= 1.
All inputs are finite; a program needn't handle non-finite values.
Results may differ from the reference program's by a relative error of at most 0.0049.
Values may be sent and summed in bfloat16 or wider, within the bound.
A program may use at most 64 MiB of HBM per device.

```python
import jax
import jax.numpy as jnp
import numpy as np
from jax import lax

HD = 128
QH = 64
KVH = 8
QG = 8
TOK_DEV = 256
TOKENS = 1024
PAGE = 64
PAGES = 16
ROWS = 256
N_CTX = 4


def folded_positions(key):
    shard_count = TOKENS // TOK_DEV
    shard_order = jax.random.permutation(jax.random.fold_in(key, 7), shard_count)
    row_index = jnp.arange(TOKENS, dtype=jnp.int32)
    shard_of = row_index // TOK_DEV
    inside = row_index % TOK_DEV
    half_rows = TOK_DEV // 2
    first_piece = shard_order[shard_of]
    piece_index = jnp.where(inside < half_rows, first_piece, 2 * shard_count - 1 - first_piece)
    return (piece_index * half_rows + inside % half_rows).astype(jnp.int32)


def draw_token_pos(key, part):
    return folded_positions(key)


def draw_page_owner(key, part):
    shard_count = TOKENS // TOK_DEV
    shard_keys = jax.random.split(jax.random.fold_in(key, 5), shard_count)

    def one_shard(shard_key):
        return jax.random.permutation(shard_key, shard_count)
    return jax.vmap(one_shard)(shard_keys).reshape(-1).astype(jnp.int32)


def draw_parents(key, part):
    upper = jnp.maximum(jnp.arange(ROWS, dtype=jnp.int32), 1)
    return jax.random.randint(jax.random.fold_in(key, 3), (ROWS,), 0, upper).astype(jnp.int32)


def draw_prefill_query(key, part):
    shape = (TOKENS, QH, HD)
    field = jnp.clip(1.5 * jax.random.normal(key, shape, jnp.float32), -6.0, 6.0)
    return field.astype(jnp.bfloat16)


def draw_prefill_keys(key, part):
    shape = (TOKENS, KVH, HD)
    leading = draw_prefill_query(key, part).astype(jnp.float32)[:, ::QG]
    field = jax.random.normal(jax.random.fold_in(key, 29), shape, jnp.float32)
    field = jnp.clip(field + 0.6 * leading, -6.0, 6.0)
    return field.astype(jnp.bfloat16)


def draw_draft_query(key, part):
    shape = (ROWS, QH, HD)
    seeded = jax.random.fold_in(key, 37)
    field = jnp.clip(1.5 * jax.random.normal(seeded, shape, jnp.float32), -6.0, 6.0)
    return field.astype(jnp.bfloat16)


def draw_draft_keys(key, part):
    shape = (ROWS, KVH, HD)
    leading = draw_draft_query(key, part).astype(jnp.float32)[:, ::QG]
    field = jax.random.normal(jax.random.fold_in(key, 31), shape, jnp.float32)
    field = jnp.clip(field + 0.6 * leading, -6.0, 6.0)
    return field.astype(jnp.bfloat16)


def plant(values, own_key, low, largest):
    place = [jax.random.randint(jax.random.fold_in(own_key, axis), (), 0, length) for axis, length in enumerate(values.shape)]
    widest = values.shape.index(max(values.shape))
    beside = place[:widest] + [(place[widest] + 1) % values.shape[widest]] + place[widest + 1:]
    return values.at[tuple(place)].set(low).at[tuple(beside)].set(largest)


def shard_levels(stream_key, extent, pieces, smallest, top_value):
    factor_of, own = 1.0, jax.random.fold_in(stream_key, 6)
    for position, blocks in pieces:
        heights = jnp.exp(jax.random.uniform(jax.random.fold_in(own, position), (blocks,), jnp.float32, smallest / len(pieces), top_value / len(pieces)))
        factor_of = factor_of * jnp.repeat(heights, extent[position] // blocks).reshape([-1 if axis == position else 1 for axis in range(len(extent))])
    return factor_of


def noise(key, dims, spread, bound, pieces=(), kind=jnp.bfloat16):
    values = spread * jax.random.normal(key, dims, jnp.float32)
    if pieces:
        values = values * shard_levels(key, dims, pieces, -0.22, 0.18)
    return jnp.clip(values, -bound, bound).astype(kind)


def setup_inputs(seed: int = 0) -> dict:
    key_list = jax.random.split(jax.random.key(seed), 11)
    return {
        "prefill_query": draw_prefill_query(jax.random.fold_in(key_list[10], 71), 0),
        "prefill_keys": draw_prefill_keys(jax.random.fold_in(key_list[10], 71), 0),
        "prefill_values": noise(key_list[2], (TOKENS, KVH, HD), 1.0, 6.0, ((0, 4), (1, 8))),
        "token_pos": draw_token_pos(jax.random.fold_in(key_list[10], 71), 0),
        "scale_exp": plant(jax.random.randint(key_list[4], (PAGES, KVH, 2), -7, -4), jax.random.fold_in(key_list[4], 1), -7, (-4) - 1).astype(jnp.int32),
        "page_owner": draw_page_owner(jax.random.fold_in(key_list[10], 71), 0),
        "draft_query": draw_draft_query(jax.random.fold_in(key_list[10], 71), 0),
        "draft_keys": draw_draft_keys(jax.random.fold_in(key_list[10], 71), 0),
        "draft_values": noise(key_list[8], (ROWS, KVH, HD), 1.0, 6.0, ((0, 2), (1, 4))),
        "parents": draw_parents(jax.random.fold_in(key_list[10], 71), 0),
    }


NEG_FILL = -1.0e30
FP_LIMIT = 448.0
LOG_TWO_E = 1.4426950408889634


def power_two(exponent):
    levels = jnp.arange(-7, -4, dtype=jnp.int32)
    table = jnp.asarray(np.array([2.0 ** level for level in range(-7, -4)], np.float32))
    return jnp.sum(jnp.where(exponent[..., None] == levels, table, jnp.float32(0.0)), axis=-1)


def ancestors(parent_rows):
    row_total = parent_rows.shape[0]
    row_index = jnp.arange(row_total, dtype=jnp.int32)
    linked = ((parent_rows[:, None] == row_index[None, :]) | (row_index[:, None] == row_index[None, :])).astype(jnp.float32)
    for _ in range(row_total.bit_length()):
        linked = jnp.minimum(jnp.dot(linked, linked, precision=lax.Precision.HIGHEST), jnp.float32(1.0))
    return linked > 0.5


def reference(prefill_query, prefill_keys, prefill_values, token_pos, scale_exp, page_owner, draft_query, draft_keys, draft_values, parents):
    scale_factor = HD ** -0.5
    head_outputs = []
    for kv_head in range(KVH):
        head_keys = prefill_keys[:, kv_head]
        head_values = prefill_values[:, kv_head]
        query_blocks = prefill_query[:, kv_head * QG:(kv_head + 1) * QG].reshape(TOKENS // TOK_DEV, TOK_DEV * QG, HD)
        place_blocks = jnp.repeat(token_pos, QG).reshape(TOKENS // TOK_DEV, TOK_DEV * QG)

        def attend_block(item, head_keys=head_keys, head_values=head_values):
            query_rows, query_places = item
            scores = scale_factor * jnp.dot(query_rows, head_keys.T, preferred_element_type=jnp.float32)
            allowed = query_places[:, None] >= token_pos[None, :]
            row_top = jnp.ceil(LOG_TWO_E * jnp.max(jnp.where(allowed, scores, NEG_FILL), axis=1, keepdims=True))
            weights = jnp.where(allowed, jnp.exp2(LOG_TWO_E * scores - row_top), jnp.float32(0.0))
            numer = jnp.dot(weights.astype(jnp.bfloat16), head_values, preferred_element_type=jnp.float32)
            return (numer / jnp.sum(weights, axis=1, keepdims=True)).astype(jnp.bfloat16)

        head_outputs.append(lax.map(attend_block, (query_blocks, place_blocks)).reshape(TOKENS, QG, HD))
    prefill_out = jnp.concatenate(head_outputs, axis=1)

    limits = FP_LIMIT * power_two(scale_exp)
    row_limits = jnp.repeat(limits, PAGE, axis=0)
    deq_keys = jnp.clip(prefill_keys.astype(jnp.float32), -row_limits[..., 0:1], row_limits[..., 0:1]).astype(jnp.bfloat16)
    deq_values = jnp.clip(prefill_values.astype(jnp.float32), -row_limits[..., 1:2], row_limits[..., 1:2]).astype(jnp.bfloat16)
    shard_index = jnp.arange(N_CTX, dtype=jnp.int32)
    owners = page_owner.reshape(N_CTX, N_CTX)
    inverse = jnp.sum(jnp.where(owners[:, None, :] == shard_index[None, :, None], shard_index[None, None, :], 0), axis=2).astype(jnp.int32)

    def relayout(dequantized):
        paged = dequantized.reshape(N_CTX, N_CTX, PAGE, KVH, HD)
        picked = paged[shard_index[:, None], inverse]
        return jnp.transpose(picked, (1, 0, 2, 3, 4)).reshape(TOKENS, KVH, HD)

    cache_keys = relayout(deq_keys)
    cache_values = relayout(deq_values)

    tree_mask = jnp.repeat(ancestors(parents), QG, axis=0)
    verify_heads = []
    for kv_head in range(KVH):
        draft_rows = draft_query[:, kv_head * QG:(kv_head + 1) * QG].reshape(ROWS * QG, HD)
        cache_scores = scale_factor * jnp.dot(draft_rows, deq_keys[:, kv_head].T, preferred_element_type=jnp.float32)
        tree_scores = scale_factor * jnp.dot(draft_rows, draft_keys[:, kv_head].T, preferred_element_type=jnp.float32)
        row_max = jnp.maximum(jnp.max(cache_scores, axis=1, keepdims=True), jnp.max(jnp.where(tree_mask, tree_scores, NEG_FILL), axis=1, keepdims=True))
        row_top = jnp.ceil(LOG_TWO_E * row_max)
        cache_weights = jnp.exp2(LOG_TWO_E * cache_scores - row_top)
        tree_weights = jnp.where(tree_mask, jnp.exp2(LOG_TWO_E * tree_scores - row_top), jnp.float32(0.0))
        numer = jnp.dot(cache_weights.astype(jnp.bfloat16), deq_values[:, kv_head], preferred_element_type=jnp.float32)
        numer = numer + jnp.dot(tree_weights.astype(jnp.bfloat16), draft_values[:, kv_head], preferred_element_type=jnp.float32)
        total = jnp.sum(cache_weights, axis=1, keepdims=True) + jnp.sum(tree_weights, axis=1, keepdims=True)
        verify_heads.append((numer / total).astype(jnp.bfloat16).reshape(ROWS, QG, HD))
    verify_out = jnp.concatenate(verify_heads, axis=1)
    return (prefill_out, cache_keys, cache_values, verify_out)
```

```python
import functools

import jax
import jax.numpy as jnp
from jax import lax
from jax.experimental import pallas as pl
from jax.experimental.pallas import tpu as pltpu
from jax.sharding import PartitionSpec as P

NEG_FILL = -1e30
FP_LIMIT = 448.0
LOG_TWO_E = 1.4426950408889634
META = 16
F32 = jnp.float32
BF16 = jnp.bfloat16
MESH = pl.DeviceIdType.MESH


def iota(shape, dim):
    return lax.broadcasted_iota(jnp.int32, shape, dim)


def dot(a, b):
    return lax.dot_general(a, b, (((1,), (0,)), ((), ())), preferred_element_type=F32)


def dot_t(a, b):
    return lax.dot_general(a, b, (((1,), (1,)), ((), ())), preferred_element_type=F32)


def one_hot(flag):
    return jnp.where(flag, F32(1.0), F32(0.0)).astype(BF16)


def tiled(array, width):
    return jnp.concatenate([array] * (width // array.shape[1]), axis=1)


def kernel(
    shards, sides, tok, groups, draft_rows, block,
    pos_ref, scale_ref, owner_ref, parents_ref,
    q_hbm, k_hbm, v_hbm, dq_hbm, dk_hbm, dv_hbm,
    out_ref, ck_ref, cv_ref, verify_ref,
    qbuf, kbuf, vbuf, tkbuf, tvbuf, mbuf, abuf, pbuf, accbuf, ckbuf, cvbuf, treebuf,
    local_sem, send_sem, recv_sem, tsend_sem, trecv_sem,
):
    me = lax.axis_index("ctx")
    my_side = lax.axis_index("side")
    width = qbuf.shape[1]
    half = tok // 2
    page = tok // shards
    share = draft_rows // shards
    tok_q = tok * groups
    own_q = share * groups
    scale = F32(LOG_TWO_E * width ** (-0.5))
    has_up = me + 1 < shards
    has_down = me > 0

    own_first = pl.multiple_of(me * own_q, own_q)
    copies = [
        pltpu.make_async_copy(k_hbm, kbuf.at[me, pl.ds(0, tok)], local_sem.at[0]),
        pltpu.make_async_copy(v_hbm, vbuf.at[me], local_sem.at[1]),
        pltpu.make_async_copy(dk_hbm, tkbuf.at[my_side], local_sem.at[2]),
        pltpu.make_async_copy(dv_hbm, tvbuf.at[my_side], local_sem.at[3]),
        pltpu.make_async_copy(q_hbm, qbuf.at[pl.ds(0, tok_q)], local_sem.at[4]),
        pltpu.make_async_copy(
            dq_hbm.at[pl.ds(own_first, own_q)], qbuf.at[pl.ds(tok_q, own_q)], local_sem.at[5]
        ),
    ]
    for copy in copies:
        copy.start()

    barrier = pltpu.get_barrier_semaphore()

    @pl.when(has_up)
    def _():
        pl.semaphore_signal(barrier, inc=1, device_id={"ctx": me + 1}, device_id_type=MESH)

    @pl.when(has_down)
    def _():
        pl.semaphore_signal(barrier, inc=1, device_id={"ctx": me - 1}, device_id_type=MESH)

    for step in range(1, sides):
        pl.semaphore_signal(
            barrier,
            inc=1,
            device_id={"side": lax.rem(my_side + step, sides)},
            device_id_type=MESH,
        )

    lane = iota((1, width), 1)
    rows = [jnp.zeros((1, width), F32) for _ in range(3)]
    for j in range(scale_ref.shape[1]):
        for i in range(2):
            e = scale_ref[i, j]
            bound = jnp.where(
                e == -7,
                F32(FP_LIMIT / 128),
                jnp.where(e == -6, F32(FP_LIMIT / 64), F32(FP_LIMIT / 32)),
            )
            rows[i] = jnp.where(lane == j, bound, rows[i])
        rows[2] = jnp.where(lane == j, owner_ref[j].astype(F32), rows[2])
    runs = [(pos_ref[i * half] // half).astype(F32) for i in range(2)]
    place = iota((META, width), 0)
    meta = jnp.zeros((META, width), F32)
    for i in range(3):
        meta = jnp.where(place == i, rows[i], meta)
    for i in range(2):
        meta = jnp.where(place == 3 + i, runs[i], meta)
    kbuf[me, pl.ds(tok, META), :] = meta.astype(BF16)

    def link(kind, shard, up):
        buf = (kbuf, vbuf)[kind]
        return pltpu.make_async_remote_copy(
            src_ref=buf.at[shard],
            dst_ref=buf.at[shard],
            send_sem=send_sem.at[kind, int(up), shard],
            recv_sem=recv_sem.at[kind, shard],
            device_id={"ctx": me + 1 if up else me - 1},
            device_id_type=MESH,
        )

    def arrive(kind, step):
        below, above = me - step, me + step

        @pl.when(below >= 0)
        def _():
            link(kind, below, False).wait_recv()

            @pl.when(has_up)
            def _():
                link(kind, below, True).start()

        @pl.when(above < shards)
        def _():
            link(kind, above, True).wait_recv()

            @pl.when(has_down)
            def _():
                link(kind, above, False).start()

    copies[0].wait()
    copies[1].wait()
    count = has_up.astype(jnp.int32) + has_down.astype(jnp.int32) + (sides - 1)
    pl.semaphore_wait(barrier, count)
    for kind in range(2):

        @pl.when(has_up)
        def _():
            link(kind, me, True).start()

        @pl.when(has_down)
        def _():
            link(kind, me, False).start()

    copies[2].wait()
    copies[3].wait()
    tree_sends = []
    for step in range(1, sides):
        for kind, buf in enumerate((tkbuf, tvbuf)):
            send = pltpu.make_async_remote_copy(
                src_ref=buf.at[my_side],
                dst_ref=buf.at[my_side],
                send_sem=tsend_sem.at[kind, step],
                recv_sem=trecv_sem.at[kind, step],
                device_id={"side": lax.rem(my_side + step, sides)},
                device_id_type=MESH,
            )
            send.start()
            tree_sends.append(send)

    q_row, q_col = iota((draft_rows, draft_rows), 0), iota((draft_rows, draft_rows), 1)
    tree = one_hot((parents_ref[...] == q_row) | (q_row == q_col))
    for _ in range((draft_rows - 1).bit_length()):
        tree = one_hot(dot(tree, tree) > 0.5)
    side_keys = tkbuf.shape[1]
    tree_keys = sides * side_keys
    mine = one_hot(
        iota((own_q, draft_rows), 1) == me * share + iota((own_q, draft_rows), 0) // groups
    )
    column = iota((draft_rows, tree_keys), 1)
    inside = column % side_keys
    source = (column // side_keys) * (side_keys // sides) + inside // sides
    spread = one_hot((source == iota((draft_rows, tree_keys), 0)) & (inside % sides == my_side))
    treebuf[...] = dot(dot_t(mine, tree).astype(BF16), spread)

    if shards > 1:
        arrive(0, 1)
        arrive(1, 1)

    page_of = one_hot(iota((tok, width), 0) // page == iota((tok, width), 1))
    ones_sq = jnp.ones((width, width), BF16)
    ones_v = jnp.ones((tok, width), BF16)

    def clipped(data, meta_rows, which):
        bound = dot(page_of * meta_rows[which : which + 1, :], ones_sq)
        return jnp.clip(data.astype(F32), -bound, bound).astype(BF16)

    def keep(meta_rows, data, target, shard):
        owner = dot_t(meta_rows, page_of)[2:3, :]
        pick = one_hot(
            (owner == me.astype(F32)) & (iota((page, tok), 1) % page == iota((page, tok), 0))
        )
        target[pl.ds(pl.multiple_of(shard * page, page), page), :] = dot(pick, data)

    def run_bias(meta_rows, own):
        wide = meta_rows.astype(F32)
        key_runs = jnp.concatenate(
            [jnp.broadcast_to(wide[3 + i : 4 + i, :1], (1, half)) for i in range(2)], axis=1
        )
        return jnp.where(key_runs < runs[own], F32(0.0), F32(NEG_FILL))

    def weigh(at, keys, bias=None, allowed=None, first=False):
        scores = dot_t(qbuf[at, :], keys) * scale
        if bias is not None:
            scores = scores + bias
        if allowed is not None:
            scores = jnp.where(allowed, scores, F32(NEG_FILL))
        top = jnp.ceil(jnp.max(scores, axis=1, keepdims=True))
        factor = None
        if first:
            new_top = jnp.broadcast_to(top, (block, width))
        else:
            old_top = mbuf[at, :]
            new_top = jnp.maximum(old_top, top)
            factor = jnp.exp2(old_top - new_top)
        mbuf[at, :] = new_top
        weights = jnp.exp2(scores - tiled(new_top, scores.shape[1])).astype(BF16)
        return factor, weights

    def add(at, factor, weights, values):
        part = dot(weights, values)
        if factor is None:
            accbuf[at, :] = part
        else:
            accbuf[at, :] = accbuf[at, :] * tiled(factor, 2 * width) + part

    def each(first, total, run):
        @pl.loop(0, total // block)
        def _(i):
            run(i, pl.ds(pl.multiple_of(first + i * block, block), block))

    half_q = half * groups

    copies[4].wait()
    own_keys = kbuf[me, pl.ds(0, tok), :]
    own_meta = kbuf[me, pl.ds(tok, META), :]
    own_values = jnp.concatenate([vbuf[me], ones_v], axis=1)
    for part in range(2):
        bias = run_bias(own_meta, part)

        def own_block(i, at, part=part, bias=bias):
            key = iota((block, tok), 1)
            query = (i * block + iota((block, tok), 0)) // groups
            allowed = ((key // half == part) & (key - part * half <= query)) | (bias > -1.0)
            factor, weights = weigh(at, own_keys, allowed=allowed, first=True)
            add(at, factor, weights, own_values)

        each(part * half_q, half_q, own_block)

    copies[5].wait()
    cache_k = clipped(own_keys, own_meta, 0)
    cache_v = clipped(vbuf[me], own_meta, 1)
    keep(own_meta, cache_k, ckbuf, me)
    keep(own_meta, cache_v, cvbuf, me)
    cache_v1 = jnp.concatenate([cache_v, ones_v], axis=1)

    def own_verify(i, at):
        factor, weights = weigh(at, cache_k, first=True)
        add(at, factor, weights, cache_v1)

    each(tok_q, own_q, own_verify)

    for send in tree_sends:
        send.wait_recv()
    all_tk = tkbuf[...].reshape(tree_keys, width)
    all_tv = jnp.concatenate(
        [tvbuf[...].reshape(tree_keys, width), jnp.ones((tree_keys, width), BF16)], axis=1
    )

    def tree_verify(i, at):
        allowed = treebuf[pl.ds(pl.multiple_of(i * block, block), block), :] > 0.5
        factor, weights = weigh(at, all_tk, allowed=allowed)
        add(at, factor, weights, all_tv)

    each(tok_q, own_q, tree_verify)

    def scores_of(shard, slot):
        keys = kbuf[shard, pl.ds(0, tok), :]
        meta_rows = kbuf[shard, pl.ds(tok, META), :]

        def run(i, at, keys=keys, bias=None):
            factor, weights = weigh(at, keys, bias=bias)
            abuf[slot, at, :] = factor
            pbuf[slot, at, :] = weights

        for part in range(2):
            each(part * half_q, half_q, functools.partial(run, bias=run_bias(meta_rows, part)))
        far_k = clipped(keys, meta_rows, 0)
        keep(meta_rows, far_k, ckbuf, shard)
        each(tok_q, own_q, functools.partial(run, keys=far_k))

    def values_of(shard, slot):
        values = vbuf[shard]
        meta_rows = kbuf[shard, pl.ds(tok, META), :]

        def run(i, at, values):
            add(at, abuf[slot, at, :], pbuf[slot, at, :], values)

        wide = jnp.concatenate([values, ones_v], axis=1)
        each(0, tok_q, functools.partial(run, values=wide))
        far_v = clipped(values, meta_rows, 1)
        keep(meta_rows, far_v, cvbuf, shard)
        far_v1 = jnp.concatenate([far_v, ones_v], axis=1)
        each(tok_q, own_q, functools.partial(run, values=far_v1))

    def both(step, run):
        @pl.loop(0, 2)
        def _(slot):
            shard = me + step * (2 * slot - 1)

            @pl.when((shard >= 0) & (shard < shards))
            def _():
                run(shard, slot)

    @pl.loop(1, shards)
    def _(step):
        both(step, scores_of)

        @pl.when(step > 1)
        def _():
            arrive(1, step)

        both(step, values_of)

        @pl.when(step + 1 < shards)
        def _():
            arrive(0, step + 1)

    def finish(target, first):
        def run(i, at):
            total = accbuf[at, :]
            to = pl.ds(pl.multiple_of(i * block, block), block)
            target[to, :] = (total[:, :width] / total[:, width:]).astype(BF16)

        return run

    each(0, tok_q, finish(out_ref, 0))
    each(tok_q, own_q, finish(verify_ref, tok_q))
    ck_ref[...] = ckbuf[...].astype(BF16)
    cv_ref[...] = cvbuf[...].astype(BF16)

    for send in tree_sends:
        send.wait_send()

    @pl.loop(0, shards)
    def _(step):
        below, above = me - step, me + step
        for kind in range(2):

            @pl.when((below >= 0) & has_up)
            def _():
                link(kind, below, True).wait_send()

            @pl.when((above < shards) & has_down)
            def _():
                link(kind, above, False).wait_send()


def body(
    shards, sides,
    prefill_query, prefill_keys, prefill_values, token_pos, scale_exp, page_owner,
    draft_query, draft_keys, draft_values, parents,
):
    tok, groups, width = prefill_query.shape
    draft_rows = draft_query.shape[0]
    own_q = draft_rows // shards * groups
    all_q = tok * groups + own_q
    side_keys = draft_keys.shape[0] * draft_keys.shape[1]
    block = min(256, own_q)
    hbm = pl.BlockSpec(memory_space=pl.ANY)
    smem = pl.BlockSpec(memory_space=pltpu.SMEM)
    vmem = pl.BlockSpec(memory_space=pltpu.VMEM)
    out, ck, cv, verify = pl.pallas_call(
        functools.partial(kernel, shards, sides, tok, groups, draft_rows, block),
        out_shape=(
            jax.ShapeDtypeStruct((tok * groups, width), BF16),
            jax.ShapeDtypeStruct((tok, width), BF16),
            jax.ShapeDtypeStruct((tok, width), BF16),
            jax.ShapeDtypeStruct((own_q, width), BF16),
        ),
        in_specs=[smem, smem, smem, vmem] + [hbm] * 6,
        out_specs=(vmem, vmem, vmem, vmem),
        scratch_shapes=[
            pltpu.VMEM((all_q, width), BF16),
            pltpu.VMEM((shards, tok + META, width), BF16),
            pltpu.VMEM((shards, tok, width), BF16),
            pltpu.VMEM((sides, side_keys, width), BF16),
            pltpu.VMEM((sides, side_keys, width), BF16),
            pltpu.VMEM((all_q, width), F32),
            pltpu.VMEM((2, all_q, width), F32),
            pltpu.VMEM((2, all_q, tok), BF16),
            pltpu.VMEM((all_q, 2 * width), F32),
            pltpu.VMEM((tok, width), F32),
            pltpu.VMEM((tok, width), F32),
            pltpu.VMEM((own_q, sides * side_keys), F32),
            pltpu.SemaphoreType.DMA((6,)),
            pltpu.SemaphoreType.DMA((2, 2, shards)),
            pltpu.SemaphoreType.DMA((2, shards)),
            pltpu.SemaphoreType.DMA((2, sides)),
            pltpu.SemaphoreType.DMA((2, sides)),
        ],
        compiler_params=pltpu.CompilerParams(
            collective_id=0, has_side_effects=True, vmem_limit_bytes=48 * 1024 * 1024
        ),
    )(
        token_pos,
        jnp.transpose(scale_exp[:, 0, :]),
        page_owner,
        parents.reshape(1, draft_rows),
        prefill_query.reshape(tok * groups, width),
        prefill_keys.reshape(tok, width),
        prefill_values.reshape(tok, width),
        draft_query.reshape(draft_rows * groups, width),
        draft_keys.reshape(side_keys, width),
        draft_values.reshape(side_keys, width),
    )
    return (
        out.reshape(tok, groups, width),
        ck.reshape(tok, 1, width),
        cv.reshape(tok, 1, width),
        verify.reshape(draft_rows // shards, groups, width),
    )


def solution(mesh):
    head_spec = P("ctx", ("head", "side"), None)
    return jax.shard_map(
        functools.partial(body, mesh.shape["ctx"], mesh.shape["side"]),
        mesh=mesh,
        in_specs=(
            head_spec,
            head_spec,
            head_spec,
            P("ctx"),
            head_spec,
            P("ctx"),
            P(None, ("head", "side"), None),
            P("side", "head", None),
            P("side", "head", None),
            P(),
        ),
        out_specs=(head_spec,) * 4,
        check_vma=False,
    )
```

```python
import functools

import jax
import jax.numpy as jnp
from jax import lax
from jax.experimental import pallas as pl
from jax.experimental.pallas import tpu as pltpu
from jax.sharding import PartitionSpec as P

NEG_FILL = -1e30
FP_LIMIT = 448.0
LOG_TWO_E = 1.4426950408889634
META = 16
F32 = jnp.float32
BF16 = jnp.bfloat16
MESH = pl.DeviceIdType.MESH


def iota(shape, dim):
    return lax.broadcasted_iota(jnp.int32, shape, dim)


def dot(a, b):
    return lax.dot_general(a, b, (((1,), (0,)), ((), ())), preferred_element_type=F32)


def dot_t(a, b):
    return lax.dot_general(a, b, (((1,), (1,)), ((), ())), preferred_element_type=F32)


def one_hot(flag):
    return jnp.where(flag, F32(1.0), F32(0.0)).astype(BF16)


def tiled(array, width):
    return jnp.concatenate([array] * (width // array.shape[1]), axis=1)


def kernel(
    shards, sides, tok, groups, draft_rows, block,
    pos_ref, scale_ref, owner_ref, parents_ref,
    q_hbm, k_hbm, v_hbm, dq_hbm, dk_hbm, dv_hbm,
    out_ref, ck_ref, cv_ref, verify_ref,
    qbuf, kbuf, vbuf, tkbuf, tvbuf, mbuf, abuf, pbuf, accbuf, ckbuf, cvbuf, treebuf,
    local_sem, send_sem, recv_sem, tsend_sem, trecv_sem,
):
    me = lax.axis_index("ctx")
    my_side = lax.axis_index("side")
    width = qbuf.shape[1]
    half = tok // 2
    page = tok // shards
    share = draft_rows // shards
    tok_q = tok * groups
    own_q = share * groups
    scale = F32(LOG_TWO_E * width ** (-0.5))
    has_up = me + 1 < shards
    has_down = me > 0

    own_first = pl.multiple_of(me * own_q, own_q)
    copies = [
        pltpu.make_async_copy(k_hbm, kbuf.at[me, pl.ds(0, tok)], local_sem.at[0]),
        pltpu.make_async_copy(v_hbm, vbuf.at[me], local_sem.at[1]),
        pltpu.make_async_copy(dk_hbm, tkbuf.at[my_side], local_sem.at[2]),
        pltpu.make_async_copy(dv_hbm, tvbuf.at[my_side], local_sem.at[3]),
        pltpu.make_async_copy(q_hbm, qbuf.at[pl.ds(0, tok_q)], local_sem.at[4]),
        pltpu.make_async_copy(
            dq_hbm.at[pl.ds(own_first, own_q)], qbuf.at[pl.ds(tok_q, own_q)], local_sem.at[5]
        ),
    ]
    for copy in copies:
        copy.start()

    barrier = pltpu.get_barrier_semaphore()

    @pl.when(has_up)
    def _():
        pl.semaphore_signal(barrier, inc=1, device_id={"ctx": me + 1}, device_id_type=MESH)

    @pl.when(has_down)
    def _():
        pl.semaphore_signal(barrier, inc=1, device_id={"ctx": me - 1}, device_id_type=MESH)

    for step in range(1, sides):
        pl.semaphore_signal(
            barrier,
            inc=1,
            device_id={"side": lax.rem(my_side + step, sides)},
            device_id_type=MESH,
        )

    lane = iota((1, width), 1)
    rows = [jnp.zeros((1, width), F32) for _ in range(3)]
    for j in range(scale_ref.shape[1]):
        for i in range(2):
            e = scale_ref[i, j]
            bound = jnp.where(
                e == -7,
                F32(FP_LIMIT / 128),
                jnp.where(e == -6, F32(FP_LIMIT / 64), F32(FP_LIMIT / 32)),
            )
            rows[i] = jnp.where(lane == j, bound, rows[i])
        rows[2] = jnp.where(lane == j, owner_ref[j].astype(F32), rows[2])
    runs = [(pos_ref[i * half] // half).astype(F32) for i in range(2)]
    place = iota((META, width), 0)
    meta = jnp.zeros((META, width), F32)
    for i in range(3):
        meta = jnp.where(place == i, rows[i], meta)
    for i in range(2):
        meta = jnp.where(place == 3 + i, runs[i], meta)
    kbuf[me, pl.ds(tok, META), :] = meta.astype(BF16)

    def link(kind, shard, up):
        buf = (kbuf, vbuf)[kind]
        return pltpu.make_async_remote_copy(
            src_ref=buf.at[shard],
            dst_ref=buf.at[shard],
            send_sem=send_sem.at[kind, int(up), shard],
            recv_sem=recv_sem.at[kind, shard],
            device_id={"ctx": me + 1 if up else me - 1},
            device_id_type=MESH,
        )

    def arrive(kind, step):
        below, above = me - step, me + step

        @pl.when(below >= 0)
        def _():
            link(kind, below, False).wait_recv()

            @pl.when(has_up)
            def _():
                link(kind, below, True).start()

        @pl.when(above < shards)
        def _():
            link(kind, above, True).wait_recv()

            @pl.when(has_down)
            def _():
                link(kind, above, False).start()

    copies[0].wait()
    copies[1].wait()
    count = has_up.astype(jnp.int32) + has_down.astype(jnp.int32) + (sides - 1)
    pl.semaphore_wait(barrier, count)
    for kind in range(2):

        @pl.when(has_up)
        def _():
            link(kind, me, True).start()

        @pl.when(has_down)
        def _():
            link(kind, me, False).start()

    copies[2].wait()
    copies[3].wait()
    tree_sends = []
    for step in range(1, sides):
        for kind, buf in enumerate((tkbuf, tvbuf)):
            send = pltpu.make_async_remote_copy(
                src_ref=buf.at[my_side],
                dst_ref=buf.at[my_side],
                send_sem=tsend_sem.at[kind, step],
                recv_sem=trecv_sem.at[kind, step],
                device_id={"side": lax.rem(my_side + step, sides)},
                device_id_type=MESH,
            )
            send.start()
            tree_sends.append(send)

    q_row, q_col = iota((draft_rows, draft_rows), 0), iota((draft_rows, draft_rows), 1)
    tree = one_hot((parents_ref[...] == q_row) | (q_row == q_col))
    for _ in range((draft_rows - 1).bit_length()):
        tree = one_hot(dot(tree, tree) > 0.5)
    side_keys = tkbuf.shape[1]
    tree_keys = sides * side_keys
    mine = one_hot(
        iota((own_q, draft_rows), 1) == me * share + iota((own_q, draft_rows), 0) // groups
    )
    column = iota((draft_rows, tree_keys), 1)
    inside = column % side_keys
    source = (column // side_keys) * (side_keys // sides) + inside // sides
    spread = one_hot((source == iota((draft_rows, tree_keys), 0)) & (inside % sides == my_side))
    treebuf[...] = dot(dot_t(mine, tree).astype(BF16), spread)

    if shards > 1:
        arrive(0, 1)
        arrive(1, 1)

    page_of = one_hot(iota((tok, width), 0) // page == iota((tok, width), 1))
    ones_sq = jnp.ones((width, width), BF16)
    ones_v = jnp.ones((tok, width), BF16)

    def clipped(data, meta_rows, which):
        bound = dot(page_of * meta_rows[which : which + 1, :], ones_sq)
        return jnp.clip(data.astype(F32), -bound, bound).astype(BF16)

    def keep(meta_rows, data, target, shard):
        owner = dot_t(meta_rows, page_of)[2:3, :]
        pick = one_hot(
            (owner == me.astype(F32)) & (iota((page, tok), 1) % page == iota((page, tok), 0))
        )
        target[pl.ds(pl.multiple_of(shard * page, page), page), :] = dot(pick, data)

    def run_bias(meta_rows, own):
        wide = meta_rows.astype(F32)
        key_runs = jnp.concatenate(
            [jnp.broadcast_to(wide[3 + i : 4 + i, :1], (1, half)) for i in range(2)], axis=1
        )
        return jnp.where(key_runs < runs[own], F32(0.0), F32(NEG_FILL))

    def weigh(at, keys, bias=None, allowed=None, first=False):
        scores = dot_t(qbuf[at, :], keys) * scale
        if bias is not None:
            scores = scores + bias
        if allowed is not None:
            scores = jnp.where(allowed, scores, F32(NEG_FILL))
        top = jnp.ceil(jnp.max(scores, axis=1, keepdims=True))
        factor = None
        if first:
            new_top = jnp.broadcast_to(top, (block, width))
        else:
            old_top = mbuf[at, :]
            new_top = jnp.maximum(old_top, top)
            factor = jnp.exp2(old_top - new_top)
        mbuf[at, :] = new_top
        weights = jnp.exp2(scores - tiled(new_top, scores.shape[1])).astype(BF16)
        return factor, weights

    def add(at, factor, weights, values):
        part = dot(weights, values)
        if factor is None:
            accbuf[at, :] = part
        else:
            accbuf[at, :] = accbuf[at, :] * tiled(factor, 2 * width) + part

    def each(first, total, run):
        for i in range(total // block):
            run(i, pl.ds(first + i * block, block))

    half_q = half * groups

    copies[4].wait()
    own_keys = kbuf[me, pl.ds(0, tok), :]
    own_meta = kbuf[me, pl.ds(tok, META), :]
    own_values = jnp.concatenate([vbuf[me], ones_v], axis=1)
    for part in range(2):
        bias = run_bias(own_meta, part)

        def own_block(i, at, part=part, bias=bias):
            key = iota((block, tok), 1)
            query = (i * block + iota((block, tok), 0)) // groups
            allowed = ((key // half == part) & (key - part * half <= query)) | (bias > -1.0)
            factor, weights = weigh(at, own_keys, allowed=allowed, first=True)
            add(at, factor, weights, own_values)

        each(part * half_q, half_q, own_block)

    copies[5].wait()
    cache_k = clipped(own_keys, own_meta, 0)
    cache_v = clipped(vbuf[me], own_meta, 1)
    keep(own_meta, cache_k, ckbuf, me)
    keep(own_meta, cache_v, cvbuf, me)
    cache_v1 = jnp.concatenate([cache_v, ones_v], axis=1)

    def own_verify(i, at):
        factor, weights = weigh(at, cache_k, first=True)
        add(at, factor, weights, cache_v1)

    each(tok_q, own_q, own_verify)

    for send in tree_sends:
        send.wait_recv()
    all_tk = tkbuf[...].reshape(tree_keys, width)
    all_tv = jnp.concatenate(
        [tvbuf[...].reshape(tree_keys, width), jnp.ones((tree_keys, width), BF16)], axis=1
    )

    def tree_verify(i, at):
        allowed = treebuf[pl.ds(i * block, block), :] > 0.5
        factor, weights = weigh(at, all_tk, allowed=allowed)
        add(at, factor, weights, all_tv)

    each(tok_q, own_q, tree_verify)

    def scores_of(shard, slot):
        keys = kbuf[shard, pl.ds(0, tok), :]
        meta_rows = kbuf[shard, pl.ds(tok, META), :]

        def run(i, at, keys=keys, bias=None):
            factor, weights = weigh(at, keys, bias=bias)
            abuf[slot, at, :] = factor
            pbuf[slot, at, :] = weights

        for part in range(2):
            each(part * half_q, half_q, functools.partial(run, bias=run_bias(meta_rows, part)))
        far_k = clipped(keys, meta_rows, 0)
        keep(meta_rows, far_k, ckbuf, shard)
        each(tok_q, own_q, functools.partial(run, keys=far_k))

    def values_of(shard, slot):
        values = vbuf[shard]
        meta_rows = kbuf[shard, pl.ds(tok, META), :]

        def run(i, at, values):
            add(at, abuf[slot, at, :], pbuf[slot, at, :], values)

        wide = jnp.concatenate([values, ones_v], axis=1)
        each(0, tok_q, functools.partial(run, values=wide))
        far_v = clipped(values, meta_rows, 1)
        keep(meta_rows, far_v, cvbuf, shard)
        far_v1 = jnp.concatenate([far_v, ones_v], axis=1)
        each(tok_q, own_q, functools.partial(run, values=far_v1))

    def both(step, run):
        @pl.loop(0, 2)
        def _(slot):
            shard = me + step * (2 * slot - 1)

            @pl.when((shard >= 0) & (shard < shards))
            def _():
                run(shard, slot)

    @pl.loop(1, shards)
    def _(step):
        both(step, scores_of)

        @pl.when(step > 1)
        def _():
            arrive(1, step)

        both(step, values_of)

        @pl.when(step + 1 < shards)
        def _():
            arrive(0, step + 1)

    def finish(i, at, target):
        total = accbuf[at, :]
        target[pl.ds(i * block, block), :] = (total[:, :width] / total[:, width:]).astype(BF16)

    each(0, tok_q, functools.partial(finish, target=out_ref))
    each(tok_q, own_q, functools.partial(finish, target=verify_ref))
    ck_ref[...] = ckbuf[...].astype(BF16)
    cv_ref[...] = cvbuf[...].astype(BF16)

    for send in tree_sends:
        send.wait_send()

    @pl.loop(0, shards)
    def _(step):
        below, above = me - step, me + step
        for kind in range(2):

            @pl.when((below >= 0) & has_up)
            def _():
                link(kind, below, True).wait_send()

            @pl.when((above < shards) & has_down)
            def _():
                link(kind, above, False).wait_send()


def body(
    shards, sides,
    prefill_query, prefill_keys, prefill_values, token_pos, scale_exp, page_owner,
    draft_query, draft_keys, draft_values, parents,
):
    tok, groups, width = prefill_query.shape
    draft_rows = draft_query.shape[0]
    own_q = draft_rows // shards * groups
    all_q = tok * groups + own_q
    side_keys = draft_keys.shape[0] * draft_keys.shape[1]
    block = min(256, own_q)
    hbm = pl.BlockSpec(memory_space=pltpu.HBM)
    smem = pl.BlockSpec(memory_space=pltpu.SMEM)
    vmem = pl.BlockSpec(memory_space=pltpu.VMEM)
    out, ck, cv, verify = pl.pallas_call(
        functools.partial(kernel, shards, sides, tok, groups, draft_rows, block),
        out_shape=(
            jax.ShapeDtypeStruct((tok * groups, width), BF16),
            jax.ShapeDtypeStruct((tok, width), BF16),
            jax.ShapeDtypeStruct((tok, width), BF16),
            jax.ShapeDtypeStruct((own_q, width), BF16),
        ),
        in_specs=[smem, smem, smem, vmem] + [hbm] * 6,
        out_specs=(vmem, vmem, vmem, vmem),
        scratch_shapes=[
            pltpu.VMEM((all_q, width), BF16),
            pltpu.VMEM((shards, tok + META, width), BF16),
            pltpu.VMEM((shards, tok, width), BF16),
            pltpu.VMEM((sides, side_keys, width), BF16),
            pltpu.VMEM((sides, side_keys, width), BF16),
            pltpu.VMEM((all_q, width), F32),
            pltpu.VMEM((2, all_q, width), F32),
            pltpu.VMEM((2, all_q, tok), BF16),
            pltpu.VMEM((all_q, 2 * width), F32),
            pltpu.VMEM((tok, width), F32),
            pltpu.VMEM((tok, width), F32),
            pltpu.VMEM((own_q, sides * side_keys), F32),
            pltpu.SemaphoreType.DMA((6,)),
            pltpu.SemaphoreType.DMA((2, 2, shards)),
            pltpu.SemaphoreType.DMA((2, shards)),
            pltpu.SemaphoreType.DMA((2, sides)),
            pltpu.SemaphoreType.DMA((2, sides)),
        ],
        compiler_params=pltpu.CompilerParams(
            collective_id=0, has_side_effects=True, vmem_limit_bytes=63 * 1024 * 1024
        ),
    )(
        token_pos,
        jnp.transpose(scale_exp[:, 0, :]),
        page_owner,
        parents.reshape(1, draft_rows),
        prefill_query.reshape(tok * groups, width),
        prefill_keys.reshape(tok, width),
        prefill_values.reshape(tok, width),
        draft_query.reshape(draft_rows * groups, width),
        draft_keys.reshape(side_keys, width),
        draft_values.reshape(side_keys, width),
    )
    return (
        out.reshape(tok, groups, width),
        ck.reshape(tok, 1, width),
        cv.reshape(tok, 1, width),
        verify.reshape(draft_rows // shards, groups, width),
    )


def solution(mesh):
    head_spec = P("ctx", ("head", "side"), None)
    return jax.shard_map(
        functools.partial(body, mesh.shape["ctx"], mesh.shape["side"]),
        mesh=mesh,
        in_specs=(
            head_spec,
            head_spec,
            head_spec,
            P("ctx"),
            head_spec,
            P("ctx"),
            P(None, ("head", "side"), None),
            P("side", "head", None),
            P("side", "head", None),
            P(),
        ),
        out_specs=(head_spec,) * 4,
        check_vma=False,
    )
```

```python
import functools

import jax
import jax.numpy as jnp
from jax import lax
from jax.experimental import pallas as pl
from jax.experimental.pallas import tpu as pltpu
from jax.sharding import PartitionSpec as P

NEG_FILL = -1e30
FP_LIMIT = 448.0
LOG_TWO_E = 1.4426950408889634
META = 16
F32 = jnp.float32
BF16 = jnp.bfloat16
MESH = pl.DeviceIdType.MESH


def iota(shape, dim):
    return lax.broadcasted_iota(jnp.int32, shape, dim)


def dot(a, b):
    return lax.dot_general(a, b, (((1,), (0,)), ((), ())), preferred_element_type=F32)


def dot_t(a, b):
    return lax.dot_general(a, b, (((1,), (1,)), ((), ())), preferred_element_type=F32)


def one_hot(flag):
    return jnp.where(flag, F32(1.0), F32(0.0)).astype(BF16)


def tiled(array, width):
    return jnp.concatenate([array] * (width // array.shape[1]), axis=1)


def kernel(
    shards, sides, tok, groups, draft_rows, block,
    pos_ref, scale_ref, owner_ref, parents_ref,
    q_hbm, k_hbm, v_hbm, dq_hbm, dk_hbm, dv_hbm,
    out_ref, ck_ref, cv_ref, verify_ref,
    qbuf, kbuf, vbuf, tkbuf, tvbuf, mbuf, accbuf, ckbuf, cvbuf, treebuf,
    local_sem, send_sem, recv_sem, tsend_sem, trecv_sem,
):
    me = lax.axis_index("ctx")
    my_side = lax.axis_index("side")
    width = qbuf.shape[1]
    half = tok // 2
    page = tok // shards
    share = draft_rows // shards
    tok_q = tok * groups
    own_q = share * groups
    scale = F32(LOG_TWO_E * width ** (-0.5))
    has_up = me + 1 < shards
    has_down = me > 0

    own_first = pl.multiple_of(me * own_q, own_q)
    copies = [
        pltpu.make_async_copy(k_hbm, kbuf.at[me, pl.ds(0, tok)], local_sem.at[0]),
        pltpu.make_async_copy(v_hbm, vbuf.at[me], local_sem.at[1]),
        pltpu.make_async_copy(dk_hbm, tkbuf.at[my_side], local_sem.at[2]),
        pltpu.make_async_copy(dv_hbm, tvbuf.at[my_side], local_sem.at[3]),
        pltpu.make_async_copy(q_hbm, qbuf.at[pl.ds(0, tok_q)], local_sem.at[4]),
        pltpu.make_async_copy(
            dq_hbm.at[pl.ds(own_first, own_q)], qbuf.at[pl.ds(tok_q, own_q)], local_sem.at[5]
        ),
    ]
    for copy in copies:
        copy.start()

    barrier = pltpu.get_barrier_semaphore()

    @pl.when(has_up)
    def _():
        pl.semaphore_signal(barrier, inc=1, device_id={"ctx": me + 1}, device_id_type=MESH)

    @pl.when(has_down)
    def _():
        pl.semaphore_signal(barrier, inc=1, device_id={"ctx": me - 1}, device_id_type=MESH)

    for step in range(1, sides):
        pl.semaphore_signal(
            barrier,
            inc=1,
            device_id={"side": lax.rem(my_side + step, sides)},
            device_id_type=MESH,
        )

    lane = iota((1, width), 1)
    rows = [jnp.zeros((1, width), F32) for _ in range(3)]
    for j in range(scale_ref.shape[1]):
        for i in range(2):
            e = scale_ref[i, j]
            bound = jnp.where(
                e == -7,
                F32(FP_LIMIT / 128),
                jnp.where(e == -6, F32(FP_LIMIT / 64), F32(FP_LIMIT / 32)),
            )
            rows[i] = jnp.where(lane == j, bound, rows[i])
        rows[2] = jnp.where(lane == j, owner_ref[j].astype(F32), rows[2])
    runs = [(pos_ref[i * half] // half).astype(F32) for i in range(2)]
    place = iota((META, width), 0)
    meta = jnp.zeros((META, width), F32)
    for i in range(3):
        meta = jnp.where(place == i, rows[i], meta)
    for i in range(2):
        meta = jnp.where(place == 3 + i, runs[i], meta)
    kbuf[me, pl.ds(tok, META), :] = meta.astype(BF16)

    def link(kind, shard, up):
        buf = (kbuf, vbuf)[kind]
        return pltpu.make_async_remote_copy(
            src_ref=buf.at[shard],
            dst_ref=buf.at[shard],
            send_sem=send_sem.at[kind, int(up), shard],
            recv_sem=recv_sem.at[kind, shard],
            device_id={"ctx": me + 1 if up else me - 1},
            device_id_type=MESH,
        )

    def arrive(kind, step):
        below, above = me - step, me + step

        @pl.when(below >= 0)
        def _():
            link(kind, below, False).wait_recv()

            @pl.when(has_up)
            def _():
                link(kind, below, True).start()

        @pl.when(above < shards)
        def _():
            link(kind, above, True).wait_recv()

            @pl.when(has_down)
            def _():
                link(kind, above, False).start()

    copies[0].wait()
    copies[1].wait()
    count = has_up.astype(jnp.int32) + has_down.astype(jnp.int32) + (sides - 1)
    pl.semaphore_wait(barrier, count)
    for kind in range(2):

        @pl.when(has_up)
        def _():
            link(kind, me, True).start()

        @pl.when(has_down)
        def _():
            link(kind, me, False).start()

    copies[2].wait()
    copies[3].wait()
    tree_sends = []
    for step in range(1, sides):
        for kind, buf in enumerate((tkbuf, tvbuf)):
            send = pltpu.make_async_remote_copy(
                src_ref=buf.at[my_side],
                dst_ref=buf.at[my_side],
                send_sem=tsend_sem.at[kind, step],
                recv_sem=trecv_sem.at[kind, step],
                device_id={"side": lax.rem(my_side + step, sides)},
                device_id_type=MESH,
            )
            send.start()
            tree_sends.append(send)

    q_row, q_col = iota((draft_rows, draft_rows), 0), iota((draft_rows, draft_rows), 1)
    tree = one_hot((parents_ref[...] == q_row) | (q_row == q_col))
    for _ in range((draft_rows - 1).bit_length()):
        tree = one_hot(dot(tree, tree) > 0.5)
    side_keys = tkbuf.shape[1]
    tree_keys = sides * side_keys
    mine = one_hot(
        iota((own_q, draft_rows), 1) == me * share + iota((own_q, draft_rows), 0) // groups
    )
    column = iota((draft_rows, tree_keys), 1)
    inside = column % side_keys
    source = (column // side_keys) * (side_keys // sides) + inside // sides
    spread = one_hot((source == iota((draft_rows, tree_keys), 0)) & (inside % sides == my_side))
    treebuf[...] = dot(dot_t(mine, tree).astype(BF16), spread)

    if shards > 1:
        arrive(0, 1)
        arrive(1, 1)

    page_of = one_hot(iota((tok, width), 0) // page == iota((tok, width), 1))
    ones_sq = jnp.ones((width, width), BF16)
    ones_v = jnp.ones((tok, width), BF16)

    def clipped(data, meta_rows, which):
        bound = dot(page_of * meta_rows[which : which + 1, :], ones_sq)
        return jnp.clip(data.astype(F32), -bound, bound).astype(BF16)

    def keep(meta_rows, data, target, shard):
        owner = dot_t(meta_rows, page_of)[2:3, :]
        pick = one_hot(
            (owner == me.astype(F32)) & (iota((page, tok), 1) % page == iota((page, tok), 0))
        )
        target[pl.ds(pl.multiple_of(shard * page, page), page), :] = dot(pick, data)

    def run_bias(meta_rows, own):
        wide = meta_rows.astype(F32)
        key_runs = jnp.concatenate(
            [jnp.broadcast_to(wide[3 + i : 4 + i, :1], (1, half)) for i in range(2)], axis=1
        )
        return jnp.where(key_runs < runs[own], F32(0.0), F32(NEG_FILL))

    def weigh(at, keys, bias=None, allowed=None, first=False):
        scores = dot_t(qbuf[at, :], keys) * scale
        if bias is not None:
            scores = scores + bias
        if allowed is not None:
            scores = jnp.where(allowed, scores, F32(NEG_FILL))
        top = jnp.ceil(jnp.max(scores, axis=1, keepdims=True))
        factor = None
        if first:
            new_top = jnp.broadcast_to(top, (block, width))
        else:
            old_top = mbuf[at, :]
            new_top = jnp.maximum(old_top, top)
            factor = jnp.exp2(old_top - new_top)
        mbuf[at, :] = new_top
        weights = jnp.exp2(scores - tiled(new_top, scores.shape[1])).astype(BF16)
        return factor, weights

    def add(at, factor, weights, values):
        part = dot(weights, values)
        if factor is None:
            accbuf[at, :] = part
        else:
            accbuf[at, :] = accbuf[at, :] * tiled(factor, 2 * width) + part

    def each(first, total, run):
        for i in range(total // block):
            run(i, pl.ds(first + i * block, block))

    half_q = half * groups

    copies[4].wait()
    own_keys = kbuf[me, pl.ds(0, tok), :]
    own_meta = kbuf[me, pl.ds(tok, META), :]
    own_values = jnp.concatenate([vbuf[me], ones_v], axis=1)
    for part in range(2):
        bias = run_bias(own_meta, part)

        def own_block(i, at, part=part, bias=bias):
            key = iota((block, tok), 1)
            query = (i * block + iota((block, tok), 0)) // groups
            allowed = ((key // half == part) & (key - part * half <= query)) | (bias > -1.0)
            factor, weights = weigh(at, own_keys, allowed=allowed, first=True)
            add(at, factor, weights, own_values)

        each(part * half_q, half_q, own_block)

    copies[5].wait()
    cache_k = clipped(own_keys, own_meta, 0)
    cache_v = clipped(vbuf[me], own_meta, 1)
    keep(own_meta, cache_k, ckbuf, me)
    keep(own_meta, cache_v, cvbuf, me)
    cache_v1 = jnp.concatenate([cache_v, ones_v], axis=1)

    def own_verify(i, at):
        factor, weights = weigh(at, cache_k, first=True)
        add(at, factor, weights, cache_v1)

    each(tok_q, own_q, own_verify)

    for send in tree_sends:
        send.wait_recv()
    all_tk = tkbuf[...].reshape(tree_keys, width)
    all_tv = jnp.concatenate(
        [tvbuf[...].reshape(tree_keys, width), jnp.ones((tree_keys, width), BF16)], axis=1
    )

    def tree_verify(i, at):
        allowed = treebuf[pl.ds(i * block, block), :] > 0.5
        factor, weights = weigh(at, all_tk, allowed=allowed)
        add(at, factor, weights, all_tv)

    each(tok_q, own_q, tree_verify)

    def attend(shard):
        keys = kbuf[shard, pl.ds(0, tok), :]
        meta_rows = kbuf[shard, pl.ds(tok, META), :]
        values = vbuf[shard]

        def run(i, at, keys, values, bias):
            factor, weights = weigh(at, keys, bias=bias)
            add(at, factor, weights, values)

        wide = jnp.concatenate([values, ones_v], axis=1)
        for part in range(2):
            bias = run_bias(meta_rows, part)
            each(
                part * half_q,
                half_q,
                functools.partial(run, keys=keys, values=wide, bias=bias),
            )
        far_k = clipped(keys, meta_rows, 0)
        far_v = clipped(values, meta_rows, 1)
        keep(meta_rows, far_k, ckbuf, shard)
        keep(meta_rows, far_v, cvbuf, shard)
        far_v1 = jnp.concatenate([far_v, ones_v], axis=1)
        each(tok_q, own_q, functools.partial(run, keys=far_k, values=far_v1, bias=None))

    @pl.loop(1, shards)
    def _(step):
        @pl.when(step + 1 < shards)
        def _():
            arrive(0, step + 1)
            arrive(1, step + 1)

        @pl.loop(0, 2)
        def _(slot):
            shard = me + step * (2 * slot - 1)

            @pl.when((shard >= 0) & (shard < shards))
            def _():
                attend(shard)

    def finish(i, at, target):
        total = accbuf[at, :]
        target[pl.ds(i * block, block), :] = (total[:, :width] / total[:, width:]).astype(BF16)

    each(0, tok_q, functools.partial(finish, target=out_ref))
    each(tok_q, own_q, functools.partial(finish, target=verify_ref))
    ck_ref[...] = ckbuf[...].astype(BF16)
    cv_ref[...] = cvbuf[...].astype(BF16)

    for send in tree_sends:
        send.wait_send()

    @pl.loop(0, shards)
    def _(step):
        below, above = me - step, me + step
        for kind in range(2):

            @pl.when((below >= 0) & has_up)
            def _():
                link(kind, below, True).wait_send()

            @pl.when((above < shards) & has_down)
            def _():
                link(kind, above, False).wait_send()


def hand_over(*refs):
    for source, target in zip(refs[:4], refs[4:]):
        target[...] = source[...]


def body(
    shards, sides,
    prefill_query, prefill_keys, prefill_values, token_pos, scale_exp, page_owner,
    draft_query, draft_keys, draft_values, parents,
):
    tok, groups, width = prefill_query.shape
    draft_rows = draft_query.shape[0]
    own_q = draft_rows // shards * groups
    all_q = tok * groups + own_q
    side_keys = draft_keys.shape[0] * draft_keys.shape[1]
    block = min(256, own_q)
    hbm = pl.BlockSpec(memory_space=pltpu.HBM)
    smem = pl.BlockSpec(memory_space=pltpu.SMEM)
    vmem = pl.BlockSpec(memory_space=pltpu.VMEM)
    out, ck, cv, verify = pl.pallas_call(
        functools.partial(kernel, shards, sides, tok, groups, draft_rows, block),
        out_shape=(
            jax.ShapeDtypeStruct((tok * groups, width), BF16),
            jax.ShapeDtypeStruct((tok, width), BF16),
            jax.ShapeDtypeStruct((tok, width), BF16),
            jax.ShapeDtypeStruct((own_q, width), BF16),
        ),
        in_specs=[smem, smem, smem, vmem] + [hbm] * 6,
        out_specs=(vmem, vmem, vmem, vmem),
        scratch_shapes=[
            pltpu.VMEM((all_q, width), BF16),
            pltpu.VMEM((shards, tok + META, width), BF16),
            pltpu.VMEM((shards, tok, width), BF16),
            pltpu.VMEM((sides, side_keys, width), BF16),
            pltpu.VMEM((sides, side_keys, width), BF16),
            pltpu.VMEM((all_q, width), F32),
            pltpu.VMEM((all_q, 2 * width), F32),
            pltpu.VMEM((tok, width), F32),
            pltpu.VMEM((tok, width), F32),
            pltpu.VMEM((own_q, sides * side_keys), F32),
            pltpu.SemaphoreType.DMA((6,)),
            pltpu.SemaphoreType.DMA((2, 2, shards)),
            pltpu.SemaphoreType.DMA((2, shards)),
            pltpu.SemaphoreType.DMA((2, sides)),
            pltpu.SemaphoreType.DMA((2, sides)),
        ],
        compiler_params=pltpu.CompilerParams(
            collective_id=0, has_side_effects=True, vmem_limit_bytes=63 * 1024 * 1024
        ),
    )(
        token_pos,
        jnp.transpose(scale_exp[:, 0, :]),
        page_owner,
        parents.reshape(1, draft_rows),
        prefill_query.reshape(tok * groups, width),
        prefill_keys.reshape(tok, width),
        prefill_values.reshape(tok, width),
        draft_query.reshape(draft_rows * groups, width),
        draft_keys.reshape(side_keys, width),
        draft_values.reshape(side_keys, width),
    )
    out, ck, cv, verify = pl.pallas_call(
        hand_over,
        out_shape=tuple(jax.ShapeDtypeStruct(x.shape, x.dtype) for x in (out, ck, cv, verify)),
        in_specs=[vmem] * 4,
        out_specs=(vmem,) * 4,
    )(out, ck, cv, verify)
    return (
        out.reshape(tok, groups, width),
        ck.reshape(tok, 1, width),
        cv.reshape(tok, 1, width),
        verify.reshape(draft_rows // shards, groups, width),
    )


def solution(mesh):
    head_spec = P("ctx", ("head", "side"), None)
    return jax.shard_map(
        functools.partial(body, mesh.shape["ctx"], mesh.shape["side"]),
        mesh=mesh,
        in_specs=(
            head_spec,
            head_spec,
            head_spec,
            P("ctx"),
            head_spec,
            P("ctx"),
            P(None, ("head", "side"), None),
            P("side", "head", None),
            P("side", "head", None),
            P(),
        ),
        out_specs=(head_spec,) * 4,
        check_vma=False,
    )
```
